256 devices in a mesh: tier: 16 (over z, core), serve: 4 (over y), head: 4 (over x).
Axes of the slice: x: 4, y: 4, z: 8, core: 2. Of those that a mesh axis runs over, the one named last changes fastest.
Arguments:
- passage_ids: int32 [16, 16], replicated, may hold values from 0 to 63, as said below
- location: int32 [64], replicated, may hold values from 0 to 63, as said below
- passage_len: int32 [64], replicated, may hold values from 128 to 256, as said below
- hit: int32 [64], P('tier'), may hold values from 0 to 1, as said below
- sel_index: int32 [16, 16, 64], P('tier'), may hold values from 0 to 255, as said below
- sel_hidden: bfloat16 [16, 1024, 8192], P('tier', None, ('serve', 'head')), may hold values from -6 to 40
- miss_hidden: bfloat16 [16, 256, 8192], P('tier', None, 'serve'), may hold values from -6 to 6
- w_qkv: bfloat16 [8192, 5120], P('serve', 'head'), may hold values from -1 to 1
- cache: bfloat16 [64, 2, 256, 512], P('tier', None, None, 'head'), may hold values from -6 to 11
Outputs:
- attended: bfloat16 [16, 16, 64, 4096], P('tier', 'serve', None, 'head')
The draws below stay inside these ranges and needn't reach their ends.
Inputs may be any that keep to these rules, and one draw needn't show every extreme that they name: `passage_ids`: within a request all ids differ; at most 2 of a request's passages are stored at one owner (location // 4), and in every request exactly 2 of them are at some owner. `location`: a permutation of the storage positions. `passage_len`: some passage has all 256 tokens live. `hit`: each owner's 4 storage positions hold exactly 1 zeros. `sel_index`: strictly increasing along the last dimension, each below the passage's live length.
All inputs are finite; a program needn't handle non-finite values.
Results may differ from the reference program's by a relative error of at most 0.018.
Values may be sent and summed in bfloat16 or wider, within the bound.
A program may use at most 128 MiB of HBM per device.

```python
import math
import jax
import jax.numpy as jnp
from jax import lax

D = 8192
HQ = 32
KVH = 4
HD = 128
G = 8
PLEN = 256
SEL = 64
NPAS = 16
MISS_DEV = 1
CAP = 2
P_OWN = 4
PASSAGES = 64
REQUESTS = 16
N_TIER = 16


def layout(key):
    key_list = jax.random.split(key, 7)
    location = jax.random.permutation(key_list[0], PASSAGES).astype(jnp.int32)
    inverse = jnp.zeros((PASSAGES,), jnp.int32).at[location].set(jnp.arange(PASSAGES, dtype=jnp.int32))
    owner_order = jax.vmap(lambda sub_key: jax.random.permutation(sub_key, N_TIER))(jax.random.split(key_list[1], REQUESTS))
    extra_tickets = jax.vmap(lambda sub_key: jax.random.permutation(sub_key, N_TIER * CAP - CAP)[:NPAS - CAP])(jax.random.split(key_list[2], REQUESTS)) + CAP
    tickets = jnp.concatenate([jnp.broadcast_to(jnp.arange(CAP), (REQUESTS, CAP)), extra_tickets], axis=1)
    group_index = tickets // CAP
    copies = tickets % CAP
    owners = jnp.take_along_axis(owner_order, group_index, axis=1)
    shifts = jax.random.randint(key_list[3], (REQUESTS, N_TIER), 0, P_OWN)
    slot_index = (copies + jnp.take_along_axis(shifts, group_index, axis=1)) % P_OWN
    stored = owners * P_OWN + slot_index
    shuffle = jax.vmap(lambda sub_key: jax.random.permutation(sub_key, NPAS))(jax.random.split(key_list[4], REQUESTS))
    passage_rows = inverse[jnp.take_along_axis(stored, shuffle, axis=1)]
    lengths = jax.random.randint(key_list[5], (PASSAGES,), PLEN // 2, PLEN + 1).at[0].set(PLEN)
    rank_scores = jax.random.randint(key_list[6], (REQUESTS, NPAS, PLEN), 0, 1 << 20) * PLEN + jnp.arange(PLEN)
    length_cut = lengths[passage_rows][..., None]
    rank_scores = jnp.where(jnp.arange(PLEN) < length_cut, rank_scores, (1 << 20) * PLEN + PLEN)
    chosen = jnp.sort(jnp.argsort(rank_scores, axis=-1)[..., :SEL], axis=-1)
    return (location, passage_rows.astype(jnp.int32), lengths.astype(jnp.int32), chosen.astype(jnp.int32))


def draw_passage_ids(key, part):
    return layout(key)[1]


def draw_location(key, part):
    return layout(key)[0]


def draw_passage_len(key, part):
    return layout(key)[2]


def draw_sel_index(key, part):
    return layout(key)[3]


def draw_hit(key, part):
    key = jax.random.fold_in(key, 11)
    orders = jax.vmap(lambda sub_key: jax.random.permutation(sub_key, P_OWN))(jax.random.split(key, N_TIER))
    return (orders >= MISS_DEV).astype(jnp.int32).reshape(PASSAGES)


def draw_w_qkv(key, part):
    key = jax.random.fold_in(key, 21)
    columns = KVH * (G + 2) * HD
    entries = jax.random.truncated_normal(key, -6.0, 6.0, (D, columns), jnp.float32) * (1.0 / math.sqrt(D))
    return entries.astype(jnp.bfloat16)


def draw_sel_hidden(key, part):
    key = jax.random.fold_in(key, 23)
    shape_all = (REQUESTS, NPAS * SEL, D)
    entries = jax.random.truncated_normal(key, -6.0, 6.0, shape_all, jnp.float32)
    return entries.astype(jnp.bfloat16)


def draw_cache(key, part):
    key = jax.random.fold_in(key, 29)
    shape_all = (PASSAGES, 2, PLEN, KVH * HD)
    entries = jax.random.truncated_normal(key, -6.0, 6.0, shape_all, jnp.float32)
    return entries.astype(jnp.bfloat16)


def shard_levels(stream_key, extent, cuts, least, top_value):
    factor_of = 1.0
    for position, parts in cuts:
        draws = jax.random.uniform(jax.random.fold_in(jax.random.fold_in(stream_key, 6), position), (parts,), jnp.float32, least / len(cuts), top_value / len(cuts))
        factor_of = factor_of * jnp.repeat(jnp.exp(draws), extent[position] // parts).reshape((-1,) + (1,) * (len(extent) - 1 - position))
    return factor_of


def bell_draw(key, dims, spread, bound, cuts=(), held_as=jnp.bfloat16):
    result = spread * jax.random.normal(key, dims, jnp.float32)
    if cuts:
        result = result * shard_levels(key, dims, cuts, -0.22, 0.18)
    return jnp.clip(result, -bound, bound).astype(held_as)


def setup_inputs(seed: int = 0) -> dict:
    keys = jax.random.split(jax.random.key(seed), 10)
    return {
        "passage_ids": draw_passage_ids(jax.random.fold_in(keys[9], 71), 0),
        "location": draw_location(jax.random.fold_in(keys[9], 71), 0),
        "passage_len": draw_passage_len(jax.random.fold_in(keys[9], 71), 0),
        "hit": draw_hit(jax.random.fold_in(keys[9], 71), 0),
        "sel_index": draw_sel_index(jax.random.fold_in(keys[9], 71), 0),
        "sel_hidden": draw_sel_hidden(jax.random.fold_in(keys[9], 71), 0),
        "miss_hidden": bell_draw(keys[6], (N_TIER * MISS_DEV, PLEN, D), 1.0, 6.0, ((0, 16), (2, 4))),
        "w_qkv": draw_w_qkv(jax.random.fold_in(keys[9], 71), 0),
        "cache": draw_cache(jax.random.fold_in(keys[9], 71), 0),
    }


def rope_parts(positions):
    half_index = jnp.arange(HD // 2, dtype=jnp.float32)
    inverse = jnp.exp(half_index * (-2.0 * math.log(500000.0) / HD))
    angle_table = positions.astype(jnp.float32)[..., None] * inverse
    return (jnp.cos(angle_table), jnp.sin(angle_table))

def rotate(values, cosine, sine_part):
    front_half = values[..., :HD // 2]
    back_half = values[..., HD // 2:]
    return jnp.concatenate([front_half * cosine - back_half * sine_part, back_half * cosine + front_half * sine_part], axis=-1)

def finish_kv(summed, positions, kv_count):
    rows_count = summed.shape[0]
    span_rows = summed.shape[1]
    row_width = kv_count * HD
    key_part = summed[..., :row_width].reshape(rows_count, span_rows, kv_count, HD)
    cosine, sine_part = rope_parts(positions)
    rotated = rotate(key_part, cosine[None, :, None, :], sine_part[None, :, None, :])
    rotated = rotated.reshape(rows_count, span_rows, row_width).astype(jnp.bfloat16)
    value_part = summed[..., row_width:].astype(jnp.bfloat16)
    return jnp.stack([rotated, value_part], axis=1)

def reference(passage_ids, location, passage_len, hit, sel_index, sel_hidden, miss_hidden, w_qkv, cache):
    row_width = KVH * HD
    weights = w_qkv.reshape(D, KVH, G + 2, HD)
    kv_weight = jnp.transpose(weights[:, :, G:, :], (0, 2, 1, 3)).reshape(D, 2 * row_width)
    summed = jnp.dot(miss_hidden.reshape(-1, D), kv_weight, preferred_element_type=jnp.float32)
    summed = summed.reshape(-1, PLEN, 2 * row_width)
    encoded = finish_kv(summed, jnp.arange(PLEN, dtype=jnp.int32), KVH)
    slot_order = jnp.argsort(hit.reshape(N_TIER, P_OWN), axis=1, stable=True)[:, :MISS_DEV]
    targets = (jnp.arange(N_TIER, dtype=jnp.int32)[:, None] * P_OWN + slot_order.astype(jnp.int32)).reshape(-1)
    kv_store = cache.at[targets].set(encoded)
    scale = 1.0 / math.sqrt(HD)
    rows_all = NPAS * SEL
    key_passage = jnp.arange(NPAS * PLEN, dtype=jnp.int32) // PLEN
    key_slot = jnp.arange(NPAS * PLEN, dtype=jnp.int32) % PLEN

    def one_request(request):
        ids_row = passage_ids[request]
        lengths = passage_len[ids_row]
        offsets = jnp.cumsum(lengths) - lengths
        blocks = kv_store[location[ids_row]]
        cached_keys = blocks[:, 0].astype(jnp.float32).reshape(NPAS, PLEN, KVH, HD)
        shift_cos, shift_sin = rope_parts(offsets)
        moved_keys = rotate(cached_keys, shift_cos[:, None, None, :], shift_sin[:, None, None, :])
        moved_keys = moved_keys.astype(jnp.bfloat16).reshape(NPAS, PLEN, row_width)
        chosen = sel_index[request]
        positions = (offsets[:, None] + chosen).reshape(-1)
        qkv = jnp.dot(sel_hidden[request], w_qkv, preferred_element_type=jnp.float32).astype(jnp.bfloat16)
        qkv = qkv.reshape(rows_all, KVH, G + 2, HD)
        cosine, sine_part = rope_parts(positions)
        queries = rotate(qkv[:, :, :G].astype(jnp.float32), cosine[:, None, None, :], sine_part[:, None, None, :]).astype(jnp.bfloat16)
        fresh_keys = rotate(qkv[:, :, G].astype(jnp.float32), cosine[:, None, :], sine_part[:, None, :]).astype(jnp.bfloat16)
        fresh_vals = qkv[:, :, G + 1]
        passage_index = jnp.arange(NPAS, dtype=jnp.int32)[:, None]
        key_table = moved_keys.at[passage_index, chosen].set(fresh_keys.reshape(NPAS, SEL, row_width))
        value_table = blocks[:, 1].at[passage_index, chosen].set(fresh_vals.reshape(NPAS, SEL, row_width))
        key_rows = key_table.reshape(NPAS * PLEN, KVH, HD)
        value_rows = value_table.reshape(NPAS * PLEN, KVH, HD)
        query_passage = jnp.arange(rows_all, dtype=jnp.int32) // SEL
        query_slot = chosen.reshape(-1)
        live = key_slot < lengths[key_passage]
        before = key_passage[None, :] < query_passage[:, None]
        same_part = (key_passage[None, :] == query_passage[:, None]) & (key_slot[None, :] <= query_slot[:, None])
        allowed = live[None, :] & (before | same_part)

        def one_head(pieces):
            query_head, key_head, value_head = pieces
            scores = jnp.einsum('qgd,kd->gqk', query_head.astype(jnp.float32), key_head.astype(jnp.float32)) * scale
            scores = jnp.where(allowed[None], scores, -jnp.inf)
            row_top = lax.optimization_barrier(jnp.max(scores, axis=-1, keepdims=True))
            expo_terms = jnp.exp(scores - row_top)
            probs = (expo_terms / lax.optimization_barrier(jnp.sum(expo_terms, axis=-1, keepdims=True))).astype(jnp.bfloat16)
            return jnp.einsum('gqk,kd->qgd', probs.astype(jnp.float32), value_head.astype(jnp.float32))
        head_out = lax.map(one_head, (jnp.moveaxis(queries, 1, 0), jnp.moveaxis(key_rows, 1, 0), jnp.moveaxis(value_rows, 1, 0)))
        attended = jnp.moveaxis(head_out, 0, 1)
        return attended.astype(jnp.bfloat16).reshape(NPAS, SEL, HQ * HD)
    return lax.map(one_request, jnp.arange(REQUESTS, dtype=jnp.int32))
```

```python
import functools
import math

import jax
import jax.numpy as jnp
from jax import lax
from jax.experimental import pallas as pl
from jax.experimental.pallas import tpu as pltpu
from jax.sharding import PartitionSpec as P

HD = 128
G = 8
PLEN = 256
SEL = 64
NPAS = 16
POWN = 4
NT = 16
NS = 4
ROWS = NPAS * SEL
COLS = (G + 2) * HD
CH = 4
CR = ROWS // CH
FEAT = 512
BF = jnp.bfloat16
F32 = jnp.float32
MESH = pl.DeviceIdType.MESH
LN_BASE = math.log(500000.0)
EXP_SCALE = math.log2(math.e) / math.sqrt(HD)


def remote(src, dst, ssem, rsem, target):
    return pltpu.make_async_remote_copy(
        src_ref=src, dst_ref=dst, send_sem=ssem, recv_sem=rsem, device_id=target, device_id_type=MESH
    )


def rope_rows(angle):
    lane = lax.broadcasted_iota(jnp.int32, angle.shape, 1)
    sine = jnp.sin(angle)
    return jnp.cos(angle), jnp.where(lane < HD // 2, -sine, sine)


def inv_freq(shape):
    lane = lax.broadcasted_iota(jnp.int32, shape, 1)
    half = jnp.where(lane < HD // 2, lane, lane - HD // 2).astype(F32)
    return jnp.exp(half * (-2.0 * LN_BASE / HD))


def rotate(x, c, s):
    return x * c + pltpu.roll(x, HD // 2, 1) * s


def kernel(
    pid_ref, loc_ref, len_ref, hit_ref, sel_ref, hid_ref, miss_ref, w_ref, cache_ref, out_ref,
    wv, mv, xb, zb, eb, er, pb, rb, fb, qb, ktab, vtab, ob, offs, oc, osn, rc, rsn, acc_s, m_s, l_s,
    lsem, xs, xr, es, ers, zs, zr, ss, sr, ps, pr, fs, fr, os_, or_,
):
    t = lax.axis_index("tier")
    s = lax.axis_index("serve")
    h = lax.axis_index("head")
    sib = {"tier": t + 1 - 2 * lax.rem(t, 2)}
    zright = {"tier": lax.rem(t + 2, NT)}
    zleft = {"tier": lax.rem(t + NT - 2, NT)}
    xright = {"head": lax.rem(h + 1, 4)}
    xleft = {"head": lax.rem(h + 3, 4)}

    def ydev(d):
        return {"serve": lax.rem(s + d, NS)}

    loads = [
        pltpu.make_async_copy(hid_ref, xb.at[0], lsem.at[0]),
        pltpu.make_async_copy(miss_ref, mv, lsem.at[1]),
        pltpu.make_async_copy(w_ref, wv, lsem.at[2]),
        pltpu.make_async_copy(cache_ref, zb.at[pl.ds(t * POWN, POWN)], lsem.at[3]),
    ]
    for cp in loads:
        cp.start()

    bar = pltpu.get_barrier_semaphore()
    partners = [xright, xleft, ydev(1), ydev(2), ydev(3), zright, zleft, sib]
    for dev in partners:
        pl.semaphore_signal(bar, inc=1, device_id=dev, device_id_type=MESH)
    pl.semaphore_wait(bar, len(partners))

    def x_own(c):
        rows = pl.ds(c * CR, CR)
        return (
            remote(xb.at[0, rows], xb.at[1, rows], xs.at[0, c], xr.at[0, c], xright),
            remote(xb.at[0, rows], xb.at[2, rows], xs.at[1, c], xr.at[1, c], xleft),
        )

    def x_fwd(c):
        a, b = pl.ds(c * CR, CR // 2), pl.ds(c * CR + CR // 2, CR // 2)
        return (
            remote(xb.at[1, a], xb.at[3, a], xs.at[2, c], xr.at[2, c], xright),
            remote(xb.at[2, b], xb.at[3, b], xs.at[3, c], xr.at[3, c], xleft),
        )

    loads[0].wait()
    for c in range(2):
        for cp in x_own(c):
            cp.start()

    total = jnp.int32(0)
    row_id = lax.broadcasted_iota(jnp.int32, (NPAS, HD), 0)
    off_rows = jnp.zeros((NPAS, HD), jnp.int32)
    for j in range(NPAS):
        offs[j] = total
        off_rows = jnp.where(row_id == j, total, off_rows)
        total = total + len_ref[pid_ref[t, j]]
    cosv, sinv = rope_rows(off_rows.astype(F32) * inv_freq((NPAS, HD)))
    oc[...] = cosv
    osn[...] = sinv

    loads[1].wait()
    loads[2].wait()
    eb[...] = jnp.dot(mv[...], wv[:, G * HD :], preferred_element_type=F32).astype(BF)
    enc = [remote(eb, er.at[d - 1], es.at[d - 1], ers.at[d - 1], ydev(d)) for d in (1, 2, 3)]
    for cp in enc:
        cp.start()

    eye = lax.broadcasted_iota(jnp.int32, (SEL, SEL), 0) == lax.broadcasted_iota(
        jnp.int32, (SEL, SEL), 1
    )
    inv64 = inv_freq((SEL, HD))

    def own_rope(c, carry):
        p = c * NS + s
        row = sel_ref[pl.ds(p, 1), :]
        col = jnp.sum(jnp.where(eye, jnp.broadcast_to(row, (SEL, SEL)), 0), axis=1, keepdims=True)
        pos = (col + offs[p]).astype(F32)
        cv, sv = rope_rows(pos * inv64)
        rc[c] = cv
        rsn[c] = sv
        return carry

    lax.fori_loop(0, CH, own_rope, 0)
    pos = lax.broadcasted_iota(jnp.int32, (PLEN, HD), 0).astype(F32)
    cosv, sinv = rope_rows(pos * inv_freq((PLEN, HD)))

    for cp in enc:
        cp.wait()
    summed = (
        eb[...].astype(F32) + er[0].astype(F32) + er[1].astype(F32) + er[2].astype(F32)
    )
    enc_k = rotate(summed[:, :HD], cosv, sinv).astype(BF)
    enc_v = summed[:, HD:].astype(BF)
    loads[3].wait()
    for i in range(POWN):
        miss = hit_ref[i] == 0
        zb[t * POWN + i, 0] = jnp.where(miss, enc_k, zb[t * POWN + i, 0])
        zb[t * POWN + i, 1] = jnp.where(miss, enc_v, zb[t * POWN + i, 1])

    def z_half(k, way, half):
        owner = lax.rem(t + 2 * NT - 2 * k if way == 0 else t + 2 * k, NT)
        return zb.at[pl.ds(owner * POWN + half * 2, 2)]

    def z_send(n, way):
        half = (n % 2) if way == 0 else 1 - (n % 2)
        ref = z_half(n // 2, way, half)
        return remote(ref, ref, zs.at[way, n], zr.at[way, n], zright if way == 0 else zleft)

    def z_recv(n, way):
        half = (n % 2) if way == 0 else 1 - (n % 2)
        ref = z_half(n // 2 + 1, way, half)
        return remote(ref, ref, zs.at[way, n], zr.at[way, n], zright if way == 0 else zleft)

    def to_sib(ref, i):
        return remote(ref, ref, ss.at[i], sr.at[i], sib)

    def sib_recv(ref, i):
        return remote(ref, ref, ss.at[i], sr.at[i], sib)

    sends = []
    sib_back = []
    sib_t = t + 1 - 2 * lax.rem(t, 2)

    def sib_ref(k, way, half):
        owner = lax.rem(sib_t + 2 * NT - 2 * k if way == 0 else sib_t + 2 * k, NT)
        return zb.at[pl.ds(owner * POWN + half * 2, 2)]

    for n in range(2):
        for way in range(2):
            cp = z_send(n, way)
            cp.start()
            sends.append(cp)
    for half in range(2):
        cp = to_sib(z_half(0, 0, half), half)
        cp.start()
        sends.append(cp)
        sib_back.append(sib_recv(sib_ref(0, 0, half), half))

    def z_service(n):
        for way in range(2):
            z_recv(n, way).wait_recv()
            half = (n % 2) if way == 0 else 1 - (n % 2)
            if n + 2 < 7:
                cp = z_send(n + 2, way)
                cp.start()
                sends.append(cp)
            i = 2 + 2 * n + way
            cp = to_sib(z_half(n // 2 + 1, way, half), i)
            cp.start()
            sends.append(cp)
            sib_back.append(sib_recv(sib_ref(n // 2 + 1, way, half), i))

    def p_send(c, d):
        rows = pl.ds(lax.rem(s + d, NS) * SEL, SEL)
        return remote(pb.at[c, rows], rb.at[c, d - 1], ps.at[c, d - 1], pr.at[c, d - 1], ydev(d))

    def project(c):
        def tile(n, carry):
            cols = pl.ds(pl.multiple_of(n * 256, 256), 256)
            total = jnp.zeros((CR, 256), F32)
            for slot, away in enumerate((0, 3, 1, 2)):
                owner = lax.rem(h + away, 4)
                wrows = pl.ds(pl.multiple_of(owner * FEAT, FEAT), FEAT)
                total += jnp.dot(
                    xb[slot, c * CR : (c + 1) * CR, :], wv[wrows, cols], preferred_element_type=F32
                )
            pb[c, :, cols] = total.astype(BF)
            return carry

        lax.fori_loop(0, COLS // 256, tile, 0)
        for d in (1, 2, 3):
            p_send(c, d).start()

    def f_send(c, d):
        slot = fb.at[c * NS + s]
        return remote(slot, slot, fs.at[c, d - 1], fr.at[c, d - 1], ydev(d))

    def f_recv(c, d):
        slot = fb.at[c * NS + lax.rem(s + NS - d, NS)]
        return remote(slot, slot, fs.at[c, d - 1], fr.at[c, d - 1], ydev(d))

    def finish_rows(c):
        for d in (1, 2, 3):
            p_send(c, d).wait()
        mine = pb[c, pl.ds(s * SEL, SEL), :].astype(F32)
        x = mine + rb[c, 0].astype(F32) + rb[c, 1].astype(F32) + rb[c, 2].astype(F32)
        x = x.astype(BF).astype(F32)
        cv, sv = rc[c], rsn[c]
        fb[c * NS + s, :, :HD] = rotate(x[:, G * HD : (G + 1) * HD], cv, sv).astype(BF)
        fb[c * NS + s, :, HD:] = x[:, (G + 1) * HD :].astype(BF)
        for d in (1, 2, 3):
            f_send(c, d).start()
        q = jnp.concatenate(
            [rotate(x[:, g * HD : (g + 1) * HD], cv, sv) for g in range(G)], axis=0
        )
        qb[c] = jnp.transpose(q).astype(BF)

    for c in range(CH):
        for cp in x_own(c):
            cp.wait()
        for cp in x_fwd(c):
            cp.start()
        if c + 2 < CH:
            for cp in x_own(c + 2):
                cp.start()
        if c >= 1:
            z_service(c - 1)
        for cp in x_fwd(c):
            cp.wait()
        project(c)
        if c >= 1:
            finish_rows(c - 1)
    z_service(3)
    finish_rows(CH - 1)
    for n in range(4, 7):
        z_service(n)
    for cp in sends:
        cp.wait_send()
    for cp in sib_back:
        cp.wait_recv()

    kio = lax.broadcasted_iota(jnp.int32, (PLEN, SEL), 0)
    kcol = lax.broadcasted_iota(jnp.int32, (PLEN, 1), 0)

    def build(j, carry):
        idx = loc_ref[pid_ref[t, j]]
        moved = rotate(zb[idx, 0].astype(F32), oc[pl.ds(j, 1), :], osn[pl.ds(j, 1), :])
        hot = (kio == sel_ref[pl.ds(j, 1), :]).astype(F32)
        chosen = jnp.max(hot, axis=1, keepdims=True) > 0.0
        fresh = jnp.dot(hot.astype(BF), fb[j], preferred_element_type=F32)
        ktab[j] = jnp.where(chosen, fresh[:, :HD], moved).astype(BF)
        vals = jnp.where(chosen, fresh[:, HD:], zb[idx, 1].astype(F32))
        vtab[j] = jnp.transpose(vals).astype(BF)
        return carry

    def o_copy(c, slot):
        return remote(ob.at[c], out_ref.at[slot], os_.at[c], or_.at[slot], {"serve": c})

    for c in range(CH):
        for d in (1, 2, 3):
            f_send(c, d).wait_send()
            f_recv(c, d).wait_recv()
        lax.fori_loop(c * NS, (c + 1) * NS, build, 0)
        p = c * NS + s
        qlim = jnp.concatenate([sel_ref[pl.ds(p, 1), :]] * G, axis=1)
        m_s[...] = jnp.full((1, G * SEL), -jnp.inf, F32)
        l_s[...] = jnp.zeros((1, G * SEL), F32)
        acc_s[...] = jnp.zeros((HD, G * SEL), F32)

        def tile(j, carry):
            sc = jnp.dot(ktab[j], qb[c], preferred_element_type=F32)
            lim = jnp.where(j < p, len_ref[pid_ref[t, j]] - 1, qlim)
            sc = jnp.where(kcol <= lim, sc, -jnp.inf)
            m_old = m_s[...]
            m_new = jnp.maximum(m_old, jnp.max(sc, axis=0, keepdims=True))
            alpha = jnp.exp2((m_old - m_new) * EXP_SCALE)
            e = jnp.exp2((sc - m_new) * EXP_SCALE)
            m_s[...] = m_new
            l_s[...] = l_s[...] * alpha + jnp.sum(e, axis=0, keepdims=True)
            acc_s[...] = acc_s[...] * alpha + jnp.dot(
                vtab[j], e.astype(BF), preferred_element_type=F32
            )
            return carry

        lax.fori_loop(0, p + 1, tile, 0)
        o = jnp.transpose(acc_s[...] / l_s[...])
        for g in range(G):
            ob[c, :, g * HD : (g + 1) * HD] = o[g * SEL : (g + 1) * SEL].astype(BF)

        @pl.when(s == c)
        def _():
            out_ref[c] = ob[c]

        @pl.when(s != c)
        def _():
            o_copy(c, s).start()

    for c in range(CH):

        @pl.when(s != c)
        def _():
            o_copy(c, s).wait_send()
            o_copy(c, c).wait_recv()


def local(
    passage_ids, location, passage_len, hit, sel_index, sel_hidden, miss_hidden, w_qkv, cache
):
    smem = pl.BlockSpec(memory_space=pltpu.SMEM)
    vmem = pl.BlockSpec(memory_space=pltpu.VMEM)
    hbm = pl.BlockSpec(memory_space=pl.ANY)
    dma = pltpu.SemaphoreType.DMA
    out = pl.pallas_call(
        kernel,
        out_shape=jax.ShapeDtypeStruct((NPAS // NS, SEL, G * HD), BF),
        in_specs=[smem, smem, smem, smem, vmem, hbm, hbm, hbm, hbm],
        out_specs=vmem,
        scratch_shapes=[
            pltpu.VMEM((4 * FEAT, COLS), BF),
            pltpu.VMEM((PLEN, 4 * FEAT), BF),
            pltpu.VMEM((4, ROWS, FEAT), BF),
            pltpu.VMEM((NT * POWN, 2, PLEN, HD), BF),
            pltpu.VMEM((PLEN, 2 * HD), BF),
            pltpu.VMEM((3, PLEN, 2 * HD), BF),
            pltpu.VMEM((CH, CR, COLS), BF),
            pltpu.VMEM((CH, 3, SEL, COLS), BF),
            pltpu.VMEM((NPAS, SEL, 2 * HD), BF),
            pltpu.VMEM((CH, HD, G * SEL), BF),
            pltpu.VMEM((NPAS, PLEN, HD), BF),
            pltpu.VMEM((NPAS, HD, PLEN), BF),
            pltpu.VMEM((CH, SEL, G * HD), BF),
            pltpu.SMEM((NPAS,), jnp.int32),
            pltpu.VMEM((NPAS, HD), F32),
            pltpu.VMEM((NPAS, HD), F32),
            pltpu.VMEM((CH, SEL, HD), F32),
            pltpu.VMEM((CH, SEL, HD), F32),
            pltpu.VMEM((HD, G * SEL), F32),
            pltpu.VMEM((1, G * SEL), F32),
            pltpu.VMEM((1, G * SEL), F32),
            dma((4,)),
            dma((4, CH)),
            dma((4, CH)),
            dma((3,)),
            dma((3,)),
            dma((2, 7)),
            dma((2, 7)),
            dma((16,)),
            dma((16,)),
            dma((CH, 3)),
            dma((CH, 3)),
            dma((CH, 3)),
            dma((CH, 3)),
            dma((CH,)),
            dma((NPAS // NS,)),
        ],
        compiler_params=pltpu.CompilerParams(
            collective_id=0, has_side_effects=True, vmem_limit_bytes=56 * 2**20
        ),
        cost_estimate=pl.CostEstimate(
            flops=10 * 10**9, bytes_accessed=9 * 2**20, transcendentals=8 * 2**20
        ),
        name="blended_attention",
    )(
        passage_ids,
        location,
        passage_len,
        hit,
        sel_index[0],
        sel_hidden[0],
        miss_hidden[0],
        w_qkv,
        cache,
    )
    return out[None]


def solution(mesh):
    in_specs = (
        P(),
        P(),
        P(),
        P("tier"),
        P("tier", None, None),
        P("tier", None, ("serve", "head")),
        P("tier", None, "serve"),
        P("serve", "head"),
        P("tier", None, None, "head"),
    )
    out_specs = P("tier", "serve", None, "head")
    return jax.shard_map(local, mesh=mesh, in_specs=in_specs, out_specs=out_specs, check_vma=False)
```

```python
import functools
import math

import jax
import jax.numpy as jnp
from jax import lax
from jax.experimental import pallas as pl
from jax.experimental.pallas import tpu as pltpu
from jax.sharding import PartitionSpec as P

HD = 128
G = 8
PLEN = 256
SEL = 64
NPAS = 16
POWN = 4
NT = 16
NS = 4
ROWS = NPAS * SEL
COLS = (G + 2) * HD
VR = HD + 16
CH = 8
CR = ROWS // CH
AHEAD = 2
SR = CR // NS
FEAT = 512
BF = jnp.bfloat16
F32 = jnp.float32
MESH = pl.DeviceIdType.MESH
LN_BASE = math.log(500000.0)
EXP_SCALE = math.log2(math.e) / math.sqrt(HD)


def remote(src, dst, ssem, rsem, target):
    return pltpu.make_async_remote_copy(
        src_ref=src, dst_ref=dst, send_sem=ssem, recv_sem=rsem, device_id=target, device_id_type=MESH
    )


def rope_rows(angle):
    lane = lax.broadcasted_iota(jnp.int32, angle.shape, 1)
    sine = jnp.sin(angle)
    return jnp.cos(angle), jnp.where(lane < HD // 2, -sine, sine)


def inv_freq(shape):
    lane = lax.broadcasted_iota(jnp.int32, shape, 1)
    half = jnp.where(lane < HD // 2, lane, lane - HD // 2).astype(F32)
    return jnp.exp(half * (-2.0 * LN_BASE / HD))


def rotate(x, c, s):
    return x * c + pltpu.roll(x, HD // 2, 1) * s


def kernel(
    pid_ref, loc_ref, len_ref, hit_ref, sel_ref, hid_ref, miss_ref, w_ref, cache_ref, out_ref,
    wv, mv, xb, cb, zb, hb, hsm, eb, er, pb, rb, fb, qb, ktab, vtab, ob, pos_s, offs, oc, osn, rc, rsn,
    acc_s, m_s,
    lsem, hs, hr, xs, xr, es, ers, zs, zr, ss, sr, ps, pr, fs, fr, os_, or_,
):
    t = lax.axis_index("tier")
    s = lax.axis_index("serve")
    h = lax.axis_index("head")
    sib = {"tier": t + 1 - 2 * lax.rem(t, 2)}
    zright = {"tier": lax.rem(t + 2, NT)}
    zleft = {"tier": lax.rem(t + NT - 2, NT)}
    xright = {"head": lax.rem(h + 1, 4)}
    xleft = {"head": lax.rem(h + 3, 4)}

    def ydev(d):
        return {"serve": lax.rem(s + d, NS)}

    loads = [
        pltpu.make_async_copy(hid_ref, xb.at[0], lsem.at[0]),
        pltpu.make_async_copy(miss_ref, mv, lsem.at[1]),
        pltpu.make_async_copy(w_ref, wv, lsem.at[2]),
        pltpu.make_async_copy(cache_ref, cb, lsem.at[3]),
    ]
    for cp in loads:
        cp.start()

    bar = pltpu.get_barrier_semaphore()
    tdev = [{"tier": lax.rem(t + d, NT)} for d in range(NT)]
    partners = [xright, xleft, ydev(1), ydev(2), ydev(3)] + tdev[1:]
    for dev in partners:
        pl.semaphore_signal(bar, inc=1, device_id=dev, device_id_type=MESH)
    pl.semaphore_wait(bar, len(partners))

    def x_own(c):
        rows = pl.ds(c * CR, CR)
        return (
            remote(xb.at[0, rows], xb.at[1, rows], xs.at[0, c], xr.at[0, c], xright),
            remote(xb.at[0, rows], xb.at[2, rows], xs.at[1, c], xr.at[1, c], xleft),
        )

    def x_fwd(c):
        a, b = pl.ds(c * CR, CR // 2), pl.ds(c * CR + CR // 2, CR // 2)
        return (
            remote(xb.at[1, a], xb.at[3, a], xs.at[2, c], xr.at[2, c], xright),
            remote(xb.at[2, b], xb.at[3, b], xs.at[3, c], xr.at[3, c], xleft),
        )

    loads[0].wait()
    for c in range(AHEAD):
        for cp in x_own(c):
            cp.start()

    missing = jnp.int32(0)
    for i in range(POWN):
        missing = missing + jnp.where(hit_ref[i] == 0, i, 0)
    hb[t] = jnp.full((1, HD), missing, jnp.int32)
    hits = [
        remote(hb.at[t], hb.at[t], hs.at[d - 1], hr.at[d - 1], tdev[d]) for d in range(1, NT)
    ]
    for cp in hits:
        cp.start()

    sib_t = t + 1 - 2 * lax.rem(t, 2)

    def z_block(me, k, way, q):
        owner = lax.rem(me + 2 * NT - 2 * k if way == 0 else me + 2 * k, NT)
        return zb.at[owner * POWN + q]

    def z_place(n, way):
        if n < 12:
            return n // 4 + 1, n % 4
        return 4, n - 12 + 2 * way

    def z_copy(k, q, way, n, ref):
        return remote(ref, ref, zs.at[way, n], zr.at[way, n], zright if way == 0 else zleft)

    sends = []
    sib_back = []

    def z_out(n, way):
        k, q = z_place(n, way)
        cp = z_copy(k, q, way, n, z_block(t, k - 1, way, q))
        cp.start()
        sends.append(cp)

    def to_sib(k, way, q, i):
        ref = z_block(t, k, way, q)
        cp = remote(ref, ref, ss.at[i], sr.at[i], sib)
        cp.start()
        sends.append(cp)
        back = z_block(sib_t, k, way, q)
        sib_back.append(remote(back, back, ss.at[i], sr.at[i], sib))

    def z_service(n):
        for way in range(2):
            k, q = z_place(n, way)
            z_copy(k, q, way, n, z_block(t, k, way, q)).wait_recv()
            if k < 3:
                z_out(n + 4, way)
            elif k == 3 and q // 2 == way:
                z_out(12 + q % 2, way)
            to_sib(k, way, q, 4 + 2 * n + way)

    loads[3].wait()
    for q in range(POWN - 1):
        zb[t * POWN + q] = cb[jnp.where(missing == q, POWN - 1, q)]
        for way in range(2):
            z_out(q, way)
    for q in range(POWN - 1):
        to_sib(0, 0, q, q)

    total = jnp.int32(0)
    row_id = lax.broadcasted_iota(jnp.int32, (NPAS, HD), 0)
    off_rows = jnp.zeros((NPAS, HD), jnp.int32)
    for j in range(NPAS):
        offs[j] = total
        off_rows = jnp.where(row_id == j, total, off_rows)
        total = total + len_ref[pid_ref[t, j]]
    cosv, sinv = rope_rows(off_rows.astype(F32) * inv_freq((NPAS, HD)))
    oc[...] = cosv
    osn[...] = sinv

    loads[1].wait()
    loads[2].wait()
    eb[...] = jnp.dot(mv[...], wv[:, G * HD :], preferred_element_type=F32).astype(BF)
    enc = [remote(eb, er.at[d - 1], es.at[d - 1], ers.at[d - 1], ydev(d)) for d in (1, 2, 3)]
    for cp in enc:
        cp.start()

    eye = lax.broadcasted_iota(jnp.int32, (SEL, SEL), 0) == lax.broadcasted_iota(
        jnp.int32, (SEL, SEL), 1
    )
    inv_rows = inv_freq((SR, HD))

    def own_rope(c, carry):
        p = 2 * c + lax.div(s, 2)
        row = sel_ref[pl.ds(p, 1), :]
        col = jnp.sum(jnp.where(eye, jnp.broadcast_to(row, (SEL, SEL)), 0), axis=1, keepdims=True)
        pos_s[...] = jnp.broadcast_to(col + offs[p], (SEL, HD))
        mine = pos_s[pl.ds(pl.multiple_of(lax.rem(s, 2) * SR, SR), SR), :]
        cv, sv = rope_rows(mine.astype(F32) * inv_rows)
        rc[c] = cv
        rsn[c] = sv
        return carry

    lax.fori_loop(0, CH, own_rope, 0)
    def finish_missing():
        pos = lax.broadcasted_iota(jnp.int32, (PLEN, HD), 0).astype(F32)
        cosv, sinv = rope_rows(pos * inv_freq((PLEN, HD)))
        for cp in enc:
            cp.wait()
        summed = eb[...].astype(F32) + er[0].astype(F32) + er[1].astype(F32) + er[2].astype(F32)
        zb[t * POWN + POWN - 1, 0] = rotate(summed[:, :HD], cosv, sinv).astype(BF)
        zb[t * POWN + POWN - 1, 1] = summed[:, HD:].astype(BF)
        for way in range(2):
            z_out(POWN - 1, way)
        to_sib(0, 0, POWN - 1, POWN - 1)

    def p_send(c, d):
        rows = pl.ds(lax.rem(s + d, NS) * SR, SR)
        return remote(pb.at[c, rows], rb.at[c, d - 1], ps.at[c, d - 1], pr.at[c, d - 1], ydev(d))

    def project(c):
        def tile(n, carry):
            cols = pl.ds(pl.multiple_of(n * 256, 256), 256)
            total = jnp.zeros((CR, 256), F32)
            for slot, away in enumerate((0, 3, 1, 2)):
                owner = lax.rem(h + away, 4)
                wrows = pl.ds(pl.multiple_of(owner * FEAT, FEAT), FEAT)
                total += jnp.dot(
                    xb[slot, c * CR : (c + 1) * CR, :], wv[wrows, cols], preferred_element_type=F32
                )
            pb[c, :, cols] = total.astype(BF)
            return carry

        lax.fori_loop(0, COLS // 256, tile, 0)
        for d in (1, 2, 3):
            p_send(c, d).start()

    def f_rows(c, who):
        return fb.at[pl.ds(pl.multiple_of(c * CR + who * SR, SR), SR)]

    def f_send(c, d):
        slot = f_rows(c, s)
        return remote(slot, slot, fs.at[c, d - 1], fr.at[c, d - 1], ydev(d))

    def f_recv(c, d):
        slot = f_rows(c, lax.rem(s + NS - d, NS))
        return remote(slot, slot, fs.at[c, d - 1], fr.at[c, d - 1], ydev(d))

    def finish_rows(c):
        for d in (1, 2, 3):
            p_send(c, d).wait()
        mine = pb[c, pl.ds(pl.multiple_of(s * SR, SR), SR), :].astype(F32)
        x = mine + rb[c, 0].astype(F32) + rb[c, 1].astype(F32) + rb[c, 2].astype(F32)
        x = x.astype(BF).astype(F32)
        cv, sv = rc[c], rsn[c]
        rows = pl.ds(pl.multiple_of(c * CR + s * SR, SR), SR)
        fb[rows, :HD] = rotate(x[:, G * HD : (G + 1) * HD], cv, sv).astype(BF)
        fb[rows, HD:] = x[:, (G + 1) * HD :].astype(BF)
        for d in (1, 2, 3):
            f_send(c, d).start()
        q = jnp.concatenate(
            [rotate(x[:, g * HD : (g + 1) * HD], cv, sv) for g in range(G)], axis=0
        )
        qb[c] = jnp.transpose(q).astype(BF)

    turns = ((), (0,), (1, 2), (3,), (4, 5), (6,), (7, 8), (9,), (10, 11))
    for i in range(CH + 1):
        if i < CH:
            for cp in x_own(i):
                cp.wait()
            for cp in x_fwd(i):
                cp.start()
            if i + AHEAD < CH:
                for cp in x_own(i + AHEAD):
                    cp.start()
        for n in turns[i]:
            z_service(n)
        if i >= 1:
            for cp in x_fwd(i - 1):
                cp.wait()
            project(i - 1)
        if i == 1:
            finish_missing()
        if i >= 2:
            finish_rows(i - 2)
    for n in (12, 13):
        z_service(n)
    for d in range(1, NT):
        hits[d - 1].wait_send()
        other = hb.at[lax.rem(t + NT - d, NT)]
        remote(other, other, hs.at[d - 1], hr.at[d - 1], tdev[d]).wait_recv()
    hit_copy = pltpu.make_async_copy(hb, hsm, lsem.at[0])
    hit_copy.start()
    for cp in sends:
        cp.wait_send()
    for cp in sib_back:
        cp.wait_recv()
    hit_copy.wait()

    kio = lax.broadcasted_iota(jnp.int32, (PLEN, SEL), 0)
    kcol = lax.broadcasted_iota(jnp.int32, (PLEN, 1), 0)
    count_row = lax.broadcasted_iota(jnp.int32, (VR - HD, PLEN), 0) == 0
    count_lane = lax.broadcasted_iota(jnp.int32, (VR - HD, PLEN), 1)

    def build(j, carry):
        pid = pid_ref[t, j]
        loc = loc_ref[pid]
        live = len_ref[pid]
        owner = lax.div(loc, POWN)
        slot = lax.rem(loc, POWN)
        gap = hsm[owner, 0, 0]
        place = jnp.where(slot == gap, POWN - 1, jnp.where(slot == POWN - 1, gap, slot))
        idx = owner * POWN + place
        half = pl.ds(pl.multiple_of(lax.rem(j, 2) * PLEN, PLEN), PLEN)
        pair = lax.div(j, 2)
        moved = rotate(zb[idx, 0].astype(F32), oc[pl.ds(j, 1), :], osn[pl.ds(j, 1), :])
        hot = (kio == sel_ref[pl.ds(j, 1), :]).astype(F32)
        chosen = jnp.max(hot, axis=1, keepdims=True) > 0.0
        rows = pl.ds(pl.multiple_of(j * SEL, SEL), SEL)
        fresh = jnp.dot(hot.astype(BF), fb[rows, :], preferred_element_type=F32)
        keys = jnp.where(chosen, fresh[:, :HD], moved)
        keys = jnp.where(kcol < live, keys, keys[0:1, :])
        ktab[pair, half, :] = keys.astype(BF)
        vals = jnp.where(chosen, fresh[:, HD:], zb[idx, 1].astype(F32))
        vals = jnp.where(kcol < live, vals, 0.0)
        vtab[pair, 0:HD, half] = jnp.transpose(vals).astype(BF)
        vtab[pair, HD:VR, half] = jnp.where(count_row & (count_lane < live), 1.0, 0.0).astype(BF)
        return carry

    def o_ref(c, who):
        rows = pl.ds(pl.multiple_of(lax.rem(who, 2) * SR, SR), SR)
        return out_ref.at[c % 2 * 2 + lax.div(who, 2), rows]

    def o_copy(c, who):
        return remote(ob.at[c], o_ref(c, who), os_.at[c], or_.at[c % 2, who], {"serve": c // 2})

    pcol = lax.broadcasted_iota(jnp.int32, (2 * PLEN, 1), 0)

    def soft_step(*steps):
        scores = [
            jnp.dot(ktab[pair], qb[c], preferred_element_type=F32) for c, pair, _ in steps
        ]
        for (c, pair, lim), sc in zip(steps, scores):
            if lim is not None:
                sc = jnp.where(pcol <= lim, sc, -jnp.inf)
            m_old = m_s[c % 2]
            m_new = jnp.maximum(m_old, jnp.max(sc, axis=0, keepdims=True))
            alpha = jnp.exp2((m_old - m_new) * EXP_SCALE)
            e = jnp.exp2((sc - m_new) * EXP_SCALE).astype(BF)
            m_s[c % 2] = m_new
            acc_s[c % 2] = acc_s[c % 2] * alpha + jnp.dot(
                vtab[pair], e, preferred_element_type=F32
            )

    def build_pair(c):
        for d in (1, 2, 3):
            f_send(c, d).wait_send()
            f_recv(c, d).wait_recv()
        lax.fori_loop(2 * c, 2 * c + 2, build, 0)

    late = lax.div(s, 2)

    def limits(c):
        row = sel_ref[pl.ds(2 * c + late, 1), :]
        lim = jnp.where(lax.rem(s, 2) == 0, row[:, :SR], row[:, SR:])
        return jnp.concatenate([lim] * G, axis=1) + late * PLEN

    def deliver(c):
        o = jnp.transpose(acc_s[c % 2, 0:HD, :] / acc_s[c % 2, HD : HD + 1, :])
        for g in range(G):
            ob[c, :, g * HD : (g + 1) * HD] = o[g * SR : (g + 1) * SR].astype(BF)

        @pl.when(s == c // 2)
        def _():
            rows = pl.ds(pl.multiple_of(lax.rem(s, 2) * SR, SR), SR)
            out_ref[c % 2 * 2 + lax.div(s, 2), rows, :] = ob[c]

        @pl.when(s != c // 2)
        def _():
            o_copy(c, s).start()

    def attend(a, before_last=None):
        b = a + 1
        m_s[...] = jnp.full((2, 1, G * SR), -jnp.inf, F32)
        acc_s[...] = jnp.zeros((2, VR, G * SR), F32)

        def both(pair, carry):
            soft_step((a, pair, None), (b, pair, None))
            return carry

        lax.fori_loop(0, a, both, 0)
        soft_step((a, a, limits(a)), (b, a, None))
        deliver(a)
        if before_last is not None:
            before_last()
        soft_step((b, b, limits(b)))
        deliver(b)

    for a in range(0, CH, 2):
        build_pair(a)
        if a == CH - 2:
            finish_rows(CH - 1)
        if a < CH - 2:
            build_pair(a + 1)
            attend(a)
        else:
            attend(a, lambda: build_pair(CH - 1))

    for c in range(CH):

        @pl.when(s != c // 2)
        def _():
            o_copy(c, s).wait_send()

    for c in range(2):
        for who in range(NS):

            @pl.when(s != who)
            def _():
                o_copy(c, who).wait_recv()


def local(
    passage_ids, location, passage_len, hit, sel_index, sel_hidden, miss_hidden, w_qkv, cache
):
    smem = pl.BlockSpec(memory_space=pltpu.SMEM)
    vmem = pl.BlockSpec(memory_space=pltpu.VMEM)
    hbm = pl.BlockSpec(memory_space=pl.ANY)
    dma = pltpu.SemaphoreType.DMA
    out = pl.pallas_call(
        kernel,
        out_shape=jax.ShapeDtypeStruct((NPAS // NS, SEL, G * HD), BF),
        in_specs=[smem, smem, smem, smem, vmem, hbm, hbm, hbm, hbm],
        out_specs=vmem,
        scratch_shapes=[
            pltpu.VMEM((4 * FEAT, COLS), BF),
            pltpu.VMEM((PLEN, 4 * FEAT), BF),
            pltpu.VMEM((4, ROWS, FEAT), BF),
            pltpu.VMEM((POWN, 2, PLEN, HD), BF),
            pltpu.VMEM((NT * POWN, 2, PLEN, HD), BF),
            pltpu.VMEM((NT, 1, HD), jnp.int32),
            pltpu.SMEM((NT, 1, HD), jnp.int32),
            pltpu.VMEM((PLEN, 2 * HD), BF),
            pltpu.VMEM((3, PLEN, 2 * HD), BF),
            pltpu.VMEM((CH, CR, COLS), BF),
            pltpu.VMEM((CH, 3, SR, COLS), BF),
            pltpu.VMEM((ROWS, 2 * HD), BF),
            pltpu.VMEM((CH, HD, G * SR), BF),
            pltpu.VMEM((NPAS // 2, 2 * PLEN, HD), BF),
            pltpu.VMEM((NPAS // 2, VR, 2 * PLEN), BF),
            pltpu.VMEM((CH, SR, G * HD), BF),
            pltpu.VMEM((SEL, HD), jnp.int32),
            pltpu.SMEM((NPAS,), jnp.int32),
            pltpu.VMEM((NPAS, HD), F32),
            pltpu.VMEM((NPAS, HD), F32),
            pltpu.VMEM((CH, SR, HD), F32),
            pltpu.VMEM((CH, SR, HD), F32),
            pltpu.VMEM((2, VR, G * SR), F32),
            pltpu.VMEM((2, 1, G * SR), F32),
            dma((4,)),
            dma((NT - 1,)),
            dma((NT - 1,)),
            dma((4, CH)),
            dma((4, CH)),
            dma((3,)),
            dma((3,)),
            dma((2, 14)),
            dma((2, 14)),
            dma((32,)),
            dma((32,)),
            dma((CH, 3)),
            dma((CH, 3)),
            dma((CH, 3)),
            dma((CH, 3)),
            dma((CH,)),
            dma((2, NS)),
        ],
        compiler_params=pltpu.CompilerParams(
            collective_id=0, has_side_effects=True, vmem_limit_bytes=56 * 2**20
        ),
        cost_estimate=pl.CostEstimate(
            flops=10 * 10**9, bytes_accessed=9 * 2**20, transcendentals=8 * 2**20
        ),
        name="blended_attention",
    )(
        passage_ids,
        location,
        passage_len,
        hit,
        sel_index[0],
        sel_hidden[0],
        miss_hidden[0],
        w_qkv,
        cache,
    )
    return out[None]


def solution(mesh):
    in_specs = (
        P(),
        P(),
        P(),
        P("tier"),
        P("tier", None, None),
        P("tier", None, ("serve", "head")),
        P("tier", None, "serve"),
        P("serve", "head"),
        P("tier", None, None, "head"),
    )
    out_specs = P("tier", "serve", None, "head")
    return jax.shard_map(local, mesh=mesh, in_specs=in_specs, out_specs=out_specs, check_vma=False)
```

```python
import functools
import math

import jax
import jax.numpy as jnp
from jax import lax
from jax.experimental import pallas as pl
from jax.experimental.pallas import tpu as pltpu
from jax.sharding import PartitionSpec as P

HD = 128
G = 8
PLEN = 256
SEL = 64
NPAS = 16
POWN = 4
NT = 16
NS = 4
ROWS = NPAS * SEL
COLS = (G + 2) * HD
VR = HD + 16
CH = 8
CR = ROWS // CH
AHEAD = 2
LAG = 3
SR = CR // NS
FEAT = 512
BF = jnp.bfloat16
F32 = jnp.float32
MESH = pl.DeviceIdType.MESH
LN_BASE = math.log(500000.0)
EXP_SCALE = math.log2(math.e) / math.sqrt(HD)


def remote(src, dst, ssem, rsem, target):
    return pltpu.make_async_remote_copy(
        src_ref=src, dst_ref=dst, send_sem=ssem, recv_sem=rsem, device_id=target, device_id_type=MESH
    )


def rope_rows(angle):
    lane = lax.broadcasted_iota(jnp.int32, angle.shape, 1)
    sine = jnp.sin(angle)
    return jnp.cos(angle), jnp.where(lane < HD // 2, -sine, sine)


def inv_freq(shape):
    lane = lax.broadcasted_iota(jnp.int32, shape, 1)
    half = jnp.where(lane < HD // 2, lane, lane - HD // 2).astype(F32)
    return jnp.exp(half * (-2.0 * LN_BASE / HD))


def rotate(x, c, s):
    return x * c + pltpu.roll(x, HD // 2, 1) * s


def kernel(
    pid_ref, loc_ref, len_ref, hit_ref, sel_ref, hid_ref, miss_ref, w_ref, cache_ref, out_ref,
    wv, mv, xb, cb, zb, hb, hsm, eb, er, pb, rb, fb, qb, ktab, vtab, ob, pos_s, offs, oc, osn, rc, rsn,
    acc_s, m_s,
    lsem, hs, hr, xs, xr, es, ers, zs, zr, ss, sr, ps, pr, fs, fr, os_, or_,
):
    t = lax.axis_index("tier")
    s = lax.axis_index("serve")
    h = lax.axis_index("head")
    sib = {"tier": t + 1 - 2 * lax.rem(t, 2)}
    zright = {"tier": lax.rem(t + 2, NT)}
    zleft = {"tier": lax.rem(t + NT - 2, NT)}
    xright = {"head": lax.rem(h + 1, 4)}
    xleft = {"head": lax.rem(h + 3, 4)}

    def ydev(d):
        return {"serve": lax.rem(s + d, NS)}

    loads = [
        pltpu.make_async_copy(hid_ref, xb.at[0], lsem.at[0]),
        pltpu.make_async_copy(miss_ref, mv, lsem.at[1]),
        pltpu.make_async_copy(w_ref, wv, lsem.at[2]),
        pltpu.make_async_copy(cache_ref, cb, lsem.at[3]),
    ]
    for cp in loads:
        cp.start()

    bar = pltpu.get_barrier_semaphore()
    tdev = [{"tier": lax.rem(t + d, NT)} for d in range(NT)]
    partners = [xright, xleft, ydev(1), ydev(2), ydev(3)] + tdev[1:]
    for dev in partners:
        pl.semaphore_signal(bar, inc=1, device_id=dev, device_id_type=MESH)
    pl.semaphore_wait(bar, len(partners))

    def x_own(c):
        rows = pl.ds(c * CR, CR)
        return (
            remote(xb.at[0, rows], xb.at[1, rows], xs.at[0, c], xr.at[0, c], xright),
            remote(xb.at[0, rows], xb.at[2, rows], xs.at[1, c], xr.at[1, c], xleft),
        )

    def x_fwd(c):
        a, b = pl.ds(c * CR, CR // 2), pl.ds(c * CR + CR // 2, CR // 2)
        return (
            remote(xb.at[1, a], xb.at[3, a], xs.at[2, c], xr.at[2, c], xright),
            remote(xb.at[2, b], xb.at[3, b], xs.at[3, c], xr.at[3, c], xleft),
        )

    loads[0].wait()
    for c in range(AHEAD):
        for cp in x_own(c):
            cp.start()

    missing = jnp.int32(0)
    for i in range(POWN):
        missing = missing + jnp.where(hit_ref[i] == 0, i, 0)
    hb[t] = jnp.full((1, HD), missing, jnp.int32)
    hits = [
        remote(hb.at[t], hb.at[t], hs.at[d - 1], hr.at[d - 1], tdev[d]) for d in range(1, NT)
    ]
    for cp in hits:
        cp.start()

    sib_t = t + 1 - 2 * lax.rem(t, 2)

    def z_block(me, k, way, q):
        owner = lax.rem(me + 2 * NT - 2 * k if way == 0 else me + 2 * k, NT)
        return zb.at[owner * POWN + q]

    def z_place(n, way):
        if n < 12:
            return n // 4 + 1, n % 4
        return 4, n - 12 + 2 * way

    def z_copy(k, q, way, n, ref):
        return remote(ref, ref, zs.at[way, n], zr.at[way, n], zright if way == 0 else zleft)

    sends = []
    sib_back = []

    def z_out(n, way):
        k, q = z_place(n, way)
        cp = z_copy(k, q, way, n, z_block(t, k - 1, way, q))
        cp.start()
        sends.append(cp)

    def to_sib(k, way, q, i):
        ref = z_block(t, k, way, q)
        cp = remote(ref, ref, ss.at[i], sr.at[i], sib)
        cp.start()
        sends.append(cp)
        back = z_block(sib_t, k, way, q)
        sib_back.append(remote(back, back, ss.at[i], sr.at[i], sib))

    def z_service(n):
        for way in range(2):
            k, q = z_place(n, way)
            z_copy(k, q, way, n, z_block(t, k, way, q)).wait_recv()
            if k < 3:
                z_out(n + 4, way)
            elif k == 3 and q // 2 == way:
                z_out(12 + q % 2, way)
            to_sib(k, way, q, 4 + 2 * n + way)

    loads[3].wait()
    for q in range(POWN - 1):
        zb[t * POWN + q] = cb[jnp.where(missing == q, POWN - 1, q)]
        for way in range(2):
            z_out(q, way)
    for q in range(POWN - 1):
        to_sib(0, 0, q, q)

    total = jnp.int32(0)
    row_id = lax.broadcasted_iota(jnp.int32, (NPAS, HD), 0)
    off_rows = jnp.zeros((NPAS, HD), jnp.int32)
    for j in range(NPAS):
        offs[j] = total
        off_rows = jnp.where(row_id == j, total, off_rows)
        total = total + len_ref[pid_ref[t, j]]
    cosv, sinv = rope_rows(off_rows.astype(F32) * inv_freq((NPAS, HD)))
    oc[...] = cosv
    osn[...] = sinv

    loads[1].wait()
    loads[2].wait()
    eb[...] = jnp.dot(mv[...], wv[:, G * HD :], preferred_element_type=F32).astype(BF)
    enc = [remote(eb, er.at[d - 1], es.at[d - 1], ers.at[d - 1], ydev(d)) for d in (1, 2, 3)]
    for cp in enc:
        cp.start()

    eye = lax.broadcasted_iota(jnp.int32, (SEL, SEL), 0) == lax.broadcasted_iota(
        jnp.int32, (SEL, SEL), 1
    )
    inv_rows = inv_freq((SR, HD))

    def own_rope(c, carry):
        p = 2 * c + lax.div(s, 2)
        row = sel_ref[pl.ds(p, 1), :]
        col = jnp.sum(jnp.where(eye, jnp.broadcast_to(row, (SEL, SEL)), 0), axis=1, keepdims=True)
        pos_s[...] = jnp.broadcast_to(col + offs[p], (SEL, HD))
        mine = pos_s[pl.ds(pl.multiple_of(lax.rem(s, 2) * SR, SR), SR), :]
        cv, sv = rope_rows(mine.astype(F32) * inv_rows)
        rc[c] = cv
        rsn[c] = sv
        return carry

    lax.fori_loop(0, CH, own_rope, 0)
    def finish_missing():
        pos = lax.broadcasted_iota(jnp.int32, (PLEN, HD), 0).astype(F32)
        cosv, sinv = rope_rows(pos * inv_freq((PLEN, HD)))
        for cp in enc:
            cp.wait()
        summed = eb[...].astype(F32) + er[0].astype(F32) + er[1].astype(F32) + er[2].astype(F32)
        zb[t * POWN + POWN - 1, 0] = rotate(summed[:, :HD], cosv, sinv).astype(BF)
        zb[t * POWN + POWN - 1, 1] = summed[:, HD:].astype(BF)
        for way in range(2):
            z_out(POWN - 1, way)
        to_sib(0, 0, POWN - 1, POWN - 1)

    def p_send(c, d):
        rows = pl.ds(lax.rem(s + d, NS) * SR, SR)
        return remote(pb.at[c, rows], rb.at[c, d - 1], ps.at[c, d - 1], pr.at[c, d - 1], ydev(d))

    def project(c):
        def tile(n, carry):
            cols = pl.ds(pl.multiple_of(n * 256, 256), 256)
            total = jnp.zeros((CR, 256), F32)
            for slot, away in enumerate((0, 3, 1, 2)):
                owner = lax.rem(h + away, 4)
                wrows = pl.ds(pl.multiple_of(owner * FEAT, FEAT), FEAT)
                total += jnp.dot(
                    xb[slot, c * CR : (c + 1) * CR, :], wv[wrows, cols], preferred_element_type=F32
                )
            pb[c, :, cols] = total.astype(BF)
            return carry

        lax.fori_loop(0, COLS // 256, tile, 0)
        for d in (1, 2, 3):
            p_send(c, d).start()

    def f_rows(c, who):
        return fb.at[pl.ds(pl.multiple_of(c * CR + who * SR, SR), SR)]

    def f_send(c, d):
        slot = f_rows(c, s)
        return remote(slot, slot, fs.at[c, d - 1], fr.at[c, d - 1], ydev(d))

    def f_recv(c, d):
        slot = f_rows(c, lax.rem(s + NS - d, NS))
        return remote(slot, slot, fs.at[c, d - 1], fr.at[c, d - 1], ydev(d))

    def finish_rows(c):
        for d in (1, 2, 3):
            p_send(c, d).wait()
        mine = pb[c, pl.ds(pl.multiple_of(s * SR, SR), SR), :].astype(F32)
        x = mine + rb[c, 0].astype(F32) + rb[c, 1].astype(F32) + rb[c, 2].astype(F32)
        x = x.astype(BF).astype(F32)
        cv, sv = rc[c], rsn[c]
        rows = pl.ds(pl.multiple_of(c * CR + s * SR, SR), SR)
        fb[rows, :HD] = rotate(x[:, G * HD : (G + 1) * HD], cv, sv).astype(BF)
        fb[rows, HD:] = x[:, (G + 1) * HD :].astype(BF)
        for d in (1, 2, 3):
            f_send(c, d).start()
        q = jnp.concatenate(
            [rotate(x[:, g * HD : (g + 1) * HD], cv, sv) for g in range(G)], axis=0
        )
        qb[c] = jnp.transpose(q).astype(BF)

    turns = ((), (0,), (1, 2), (3, 4), (5,), (6, 7), (8, 9), (10, 11), (12,))
    for i in range(CH + 1):
        if i < CH:
            for cp in x_own(i):
                cp.wait()
            for cp in x_fwd(i):
                cp.start()
            if i + AHEAD < CH:
                for cp in x_own(i + AHEAD):
                    cp.start()
        for n in turns[i]:
            z_service(n)
        if i >= 1:
            for cp in x_fwd(i - 1):
                cp.wait()
            project(i - 1)
        if i == 1:
            finish_missing()
        if i >= LAG:
            finish_rows(i - LAG)
    for c in range(CH - LAG + 1, CH - 1):
        finish_rows(c)
    z_service(13)
    finish_rows(CH - 1)
    for d in range(1, NT):
        hits[d - 1].wait_send()
        other = hb.at[lax.rem(t + NT - d, NT)]
        remote(other, other, hs.at[d - 1], hr.at[d - 1], tdev[d]).wait_recv()
    hit_copy = pltpu.make_async_copy(hb, hsm, lsem.at[0])
    hit_copy.start()
    for cp in sends:
        cp.wait_send()
    for cp in sib_back:
        cp.wait_recv()
    hit_copy.wait()

    kio = lax.broadcasted_iota(jnp.int32, (PLEN, SEL), 0)
    kcol = lax.broadcasted_iota(jnp.int32, (PLEN, 1), 0)
    count_row = lax.broadcasted_iota(jnp.int32, (VR - HD, PLEN), 0) == 0
    count_lane = lax.broadcasted_iota(jnp.int32, (VR - HD, PLEN), 1)

    def build(j, carry):
        pid = pid_ref[t, j]
        loc = loc_ref[pid]
        live = len_ref[pid]
        owner = lax.div(loc, POWN)
        slot = lax.rem(loc, POWN)
        gap = hsm[owner, 0, 0]
        place = jnp.where(slot == gap, POWN - 1, jnp.where(slot == POWN - 1, gap, slot))
        idx = owner * POWN + place
        half = pl.ds(pl.multiple_of(lax.rem(j, 2) * PLEN, PLEN), PLEN)
        pair = lax.div(j, 2)
        moved = rotate(zb[idx, 0].astype(F32), oc[pl.ds(j, 1), :], osn[pl.ds(j, 1), :])
        hot = (kio == sel_ref[pl.ds(j, 1), :]).astype(F32)
        chosen = jnp.max(hot, axis=1, keepdims=True) > 0.0
        rows = pl.ds(pl.multiple_of(j * SEL, SEL), SEL)
        fresh = jnp.dot(hot.astype(BF), fb[rows, :], preferred_element_type=F32)
        keys = jnp.where(chosen, fresh[:, :HD], moved)
        keys = jnp.where(kcol < live, keys, keys[0:1, :])
        ktab[pair, half, :] = keys.astype(BF)
        vals = jnp.where(chosen, fresh[:, HD:], zb[idx, 1].astype(F32))
        vals = jnp.where(kcol < live, vals, 0.0)
        vtab[pair, 0:HD, half] = jnp.transpose(vals).astype(BF)
        vtab[pair, HD:VR, half] = jnp.where(count_row & (count_lane < live), 1.0, 0.0).astype(BF)
        return carry

    def o_ref(c, who):
        rows = pl.ds(pl.multiple_of(lax.rem(who, 2) * SR, SR), SR)
        return out_ref.at[c % 2 * 2 + lax.div(who, 2), rows]

    def o_copy(c, who):
        return remote(ob.at[c], o_ref(c, who), os_.at[c], or_.at[c % 2, who], {"serve": c // 2})

    pcol = lax.broadcasted_iota(jnp.int32, (2 * PLEN, 1), 0)

    def soft_step(*steps):
        scores = [
            jnp.dot(ktab[pair], qb[c], preferred_element_type=F32) for _, c, pair, _ in steps
        ]
        for (slot, _, pair, lim), sc in zip(steps, scores):
            if lim is not None:
                sc = jnp.where(pcol <= lim, sc, -jnp.inf)
            m_old = m_s[slot]
            m_new = jnp.maximum(m_old, jnp.max(sc, axis=0, keepdims=True))
            alpha = jnp.exp2((m_old - m_new) * EXP_SCALE)
            e = jnp.exp2((sc - m_new) * EXP_SCALE).astype(BF)
            m_s[slot] = m_new
            acc_s[slot] = acc_s[slot] * alpha + jnp.dot(
                vtab[pair], e, preferred_element_type=F32
            )

    def build_pair(c):
        for d in (1, 2, 3):
            f_send(c, d).wait_send()
            f_recv(c, d).wait_recv()
        lax.fori_loop(2 * c, 2 * c + 2, build, 0)

    late = lax.div(s, 2)

    def limits(c):
        row = sel_ref[pl.ds(2 * c + late, 1), :]
        lim = jnp.where(lax.rem(s, 2) == 0, row[:, :SR], row[:, SR:])
        return jnp.concatenate([lim] * G, axis=1) + late * PLEN

    def deliver(c, acc):
        o = jnp.transpose(acc[0:HD, :] / acc[HD : HD + 1, :])
        for g in range(G):
            ob[c, :, g * HD : (g + 1) * HD] = o[g * SR : (g + 1) * SR].astype(BF)

        @pl.when(s == c // 2)
        def _():
            rows = pl.ds(pl.multiple_of(lax.rem(s, 2) * SR, SR), SR)
            out_ref[c % 2 * 2 + lax.div(s, 2), rows, :] = ob[c]

        @pl.when(s != c // 2)
        def _():
            o_copy(c, s).start()

    def clear():
        m_s[...] = jnp.full((8, 1, G * SR), -jnp.inf, F32)
        acc_s[...] = jnp.zeros((8, VR, G * SR), F32)

    def attend(first, last):
        chunks = range(first, last + 1)
        clear()

        def common(pair, carry):
            soft_step(*[(c - first, c, pair, None) for c in chunks])
            return carry

        lax.fori_loop(0, first, common, 0)
        for pair in chunks:
            build_pair(pair)
            soft_step(
                *[
                    (c - first, c, pair, limits(c) if c == pair else None)
                    for c in range(pair, last + 1)
                ]
            )
            deliver(pair, acc_s[pair - first])

    attend(0, 7)

    for c in range(CH):

        @pl.when(s != c // 2)
        def _():
            o_copy(c, s).wait_send()

    for c in range(2):
        for who in range(NS):

            @pl.when(s != who)
            def _():
                o_copy(c, who).wait_recv()


def local(
    passage_ids, location, passage_len, hit, sel_index, sel_hidden, miss_hidden, w_qkv, cache
):
    smem = pl.BlockSpec(memory_space=pltpu.SMEM)
    vmem = pl.BlockSpec(memory_space=pltpu.VMEM)
    hbm = pl.BlockSpec(memory_space=pl.ANY)
    dma = pltpu.SemaphoreType.DMA
    out = pl.pallas_call(
        kernel,
        out_shape=jax.ShapeDtypeStruct((NPAS // NS, SEL, G * HD), BF),
        in_specs=[smem, smem, smem, smem, vmem, hbm, hbm, hbm, hbm],
        out_specs=vmem,
        scratch_shapes=[
            pltpu.VMEM((4 * FEAT, COLS), BF),
            pltpu.VMEM((PLEN, 4 * FEAT), BF),
            pltpu.VMEM((4, ROWS, FEAT), BF),
            pltpu.VMEM((POWN, 2, PLEN, HD), BF),
            pltpu.VMEM((NT * POWN, 2, PLEN, HD), BF),
            pltpu.VMEM((NT, 1, HD), jnp.int32),
            pltpu.SMEM((NT, 1, HD), jnp.int32),
            pltpu.VMEM((PLEN, 2 * HD), BF),
            pltpu.VMEM((3, PLEN, 2 * HD), BF),
            pltpu.VMEM((CH, CR, COLS), BF),
            pltpu.VMEM((CH, 3, SR, COLS), BF),
            pltpu.VMEM((ROWS, 2 * HD), BF),
            pltpu.VMEM((CH, HD, G * SR), BF),
            pltpu.VMEM((NPAS // 2, 2 * PLEN, HD), BF),
            pltpu.VMEM((NPAS // 2, VR, 2 * PLEN), BF),
            pltpu.VMEM((CH, SR, G * HD), BF),
            pltpu.VMEM((SEL, HD), jnp.int32),
            pltpu.SMEM((NPAS,), jnp.int32),
            pltpu.VMEM((NPAS, HD), F32),
            pltpu.VMEM((NPAS, HD), F32),
            pltpu.VMEM((CH, SR, HD), F32),
            pltpu.VMEM((CH, SR, HD), F32),
            pltpu.VMEM((8, VR, G * SR), F32),
            pltpu.VMEM((8, 1, G * SR), F32),
            dma((4,)),
            dma((NT - 1,)),
            dma((NT - 1,)),
            dma((4, CH)),
            dma((4, CH)),
            dma((3,)),
            dma((3,)),
            dma((2, 14)),
            dma((2, 14)),
            dma((32,)),
            dma((32,)),
            dma((CH, 3)),
            dma((CH, 3)),
            dma((CH, 3)),
            dma((CH, 3)),
            dma((CH,)),
            dma((2, NS)),
        ],
        compiler_params=pltpu.CompilerParams(
            collective_id=0, has_side_effects=True, vmem_limit_bytes=56 * 2**20
        ),
        cost_estimate=pl.CostEstimate(
            flops=10 * 10**9, bytes_accessed=9 * 2**20, transcendentals=8 * 2**20
        ),
        name="blended_attention",
    )(
        passage_ids,
        location,
        passage_len,
        hit,
        sel_index[0],
        sel_hidden[0],
        miss_hidden[0],
        w_qkv,
        cache,
    )
    return out[None]


def solution(mesh):
    in_specs = (
        P(),
        P(),
        P(),
        P("tier"),
        P("tier", None, None),
        P("tier", None, ("serve", "head")),
        P("tier", None, "serve"),
        P("serve", "head"),
        P("tier", None, None, "head"),
    )
    out_specs = P("tier", "serve", None, "head")
    return jax.shard_map(local, mesh=mesh, in_specs=in_specs, out_specs=out_specs, check_vma=False)
```

```python
import functools
import math

import jax
import jax.numpy as jnp
from jax import lax
from jax.experimental import pallas as pl
from jax.experimental.pallas import tpu as pltpu
from jax.sharding import PartitionSpec as P

HD = 128
G = 8
PLEN = 256
SEL = 64
NPAS = 16
POWN = 4
NT = 16
NS = 4
ROWS = NPAS * SEL
COLS = (G + 2) * HD
VR = HD + 16
CH = 8
CR = ROWS // CH
AHEAD = 2
LAG = 3
SR = CR // NS
FEAT = 512
BF = jnp.bfloat16
F32 = jnp.float32
MESH = pl.DeviceIdType.MESH
LN_BASE = math.log(500000.0)
EXP_SCALE = math.log2(math.e) / math.sqrt(HD)


def remote(src, dst, ssem, rsem, target):
    return pltpu.make_async_remote_copy(
        src_ref=src, dst_ref=dst, send_sem=ssem, recv_sem=rsem, device_id=target, device_id_type=MESH
    )


def rope_rows(angle):
    lane = lax.broadcasted_iota(jnp.int32, angle.shape, 1)
    sine = jnp.sin(angle)
    return jnp.cos(angle), jnp.where(lane < HD // 2, -sine, sine)


def inv_freq(shape):
    lane = lax.broadcasted_iota(jnp.int32, shape, 1)
    half = jnp.where(lane < HD // 2, lane, lane - HD // 2).astype(F32)
    return jnp.exp(half * (-2.0 * LN_BASE / HD))


def rotate(x, c, s):
    return x * c + pltpu.roll(x, HD // 2, 1) * s


def kernel(
    pid_ref, loc_ref, len_ref, hit_ref, sel_ref, hid_ref, miss_ref, w_ref, cache_ref, out_ref,
    wv, mv, xb, cb, zb, hb, hsm, eb, er, pb, rb, fb, qb, ktab, vtab, ob, pos_s, offs, oc, osn, rc, rsn,
    acc_s, m_s,
    lsem, hs, hr, xs, xr, es, ers, zs, zr, ss, sr, ps, pr, fs, fr, os_, or_,
):
    t = lax.axis_index("tier")
    s = lax.axis_index("serve")
    h = lax.axis_index("head")
    sib = {"tier": t + 1 - 2 * lax.rem(t, 2)}
    zright = {"tier": lax.rem(t + 2, NT)}
    zleft = {"tier": lax.rem(t + NT - 2, NT)}
    xright = {"head": lax.rem(h + 1, 4)}
    xleft = {"head": lax.rem(h + 3, 4)}

    def ydev(d):
        return {"serve": lax.rem(s + d, NS)}

    loads = [
        pltpu.make_async_copy(hid_ref, xb.at[0], lsem.at[0]),
        pltpu.make_async_copy(miss_ref, mv, lsem.at[1]),
        pltpu.make_async_copy(w_ref, wv, lsem.at[2]),
        pltpu.make_async_copy(cache_ref, cb, lsem.at[3]),
    ]
    for cp in loads:
        cp.start()

    bar = pltpu.get_barrier_semaphore()
    tdev = [{"tier": lax.rem(t + d, NT)} for d in range(NT)]
    partners = [xright, xleft, ydev(1), ydev(2), ydev(3)] + tdev[1:]
    for dev in partners:
        pl.semaphore_signal(bar, inc=1, device_id=dev, device_id_type=MESH)
    pl.semaphore_wait(bar, len(partners))

    def x_own(c):
        rows = pl.ds(c * CR, CR)
        return (
            remote(xb.at[0, rows], xb.at[1, rows], xs.at[0, c], xr.at[0, c], xright),
            remote(xb.at[0, rows], xb.at[2, rows], xs.at[1, c], xr.at[1, c], xleft),
        )

    def x_fwd(c):
        a, b = pl.ds(c * CR, CR // 2), pl.ds(c * CR + CR // 2, CR // 2)
        return (
            remote(xb.at[1, a], xb.at[3, a], xs.at[2, c], xr.at[2, c], xright),
            remote(xb.at[2, b], xb.at[3, b], xs.at[3, c], xr.at[3, c], xleft),
        )

    loads[0].wait()
    for c in range(AHEAD):
        for cp in x_own(c):
            cp.start()

    missing = jnp.int32(0)
    for i in range(POWN):
        missing = missing + jnp.where(hit_ref[i] == 0, i, 0)
    hb[t] = jnp.full((1, HD), missing, jnp.int32)
    hits = [
        remote(hb.at[t], hb.at[t], hs.at[d - 1], hr.at[d - 1], tdev[d]) for d in range(1, NT)
    ]
    for cp in hits:
        cp.start()

    sib_t = t + 1 - 2 * lax.rem(t, 2)

    def z_block(me, k, way, q):
        owner = lax.rem(me + 2 * NT - 2 * k if way == 0 else me + 2 * k, NT)
        return zb.at[owner * POWN + q]

    def z_place(n, way):
        if n < 12:
            return n // 4 + 1, n % 4
        return 4, n - 12 + 2 * way

    def z_copy(k, q, way, n, ref):
        return remote(ref, ref, zs.at[way, n], zr.at[way, n], zright if way == 0 else zleft)

    sends = []
    sib_back = []

    def z_out(n, way):
        k, q = z_place(n, way)
        cp = z_copy(k, q, way, n, z_block(t, k - 1, way, q))
        cp.start()
        sends.append(cp)

    def to_sib(k, way, q, i):
        ref = z_block(t, k, way, q)
        cp = remote(ref, ref, ss.at[i], sr.at[i], sib)
        cp.start()
        sends.append(cp)
        back = z_block(sib_t, k, way, q)
        sib_back.append(remote(back, back, ss.at[i], sr.at[i], sib))

    def z_service(n):
        for way in range(2):
            k, q = z_place(n, way)
            z_copy(k, q, way, n, z_block(t, k, way, q)).wait_recv()
            if k < 3:
                z_out(n + 4, way)
            elif k == 3 and q // 2 == way:
                z_out(12 + q % 2, way)
            to_sib(k, way, q, 4 + 2 * n + way)

    loads[3].wait()
    for q in range(POWN - 1):
        zb[t * POWN + q] = cb[jnp.where(missing == q, POWN - 1, q)]
        for way in range(2):
            z_out(q, way)
    for q in range(POWN - 1):
        to_sib(0, 0, q, q)

    total = jnp.int32(0)
    row_id = lax.broadcasted_iota(jnp.int32, (NPAS, HD), 0)
    off_rows = jnp.zeros((NPAS, HD), jnp.int32)
    for j in range(NPAS):
        offs[j] = total
        off_rows = jnp.where(row_id == j, total, off_rows)
        total = total + len_ref[pid_ref[t, j]]
    cosv, sinv = rope_rows(off_rows.astype(F32) * inv_freq((NPAS, HD)))
    oc[...] = cosv
    osn[...] = sinv

    loads[1].wait()
    loads[2].wait()
    eb[...] = jnp.dot(mv[...], wv[:, G * HD :], preferred_element_type=F32).astype(BF)
    enc = [remote(eb, er.at[d - 1], es.at[d - 1], ers.at[d - 1], ydev(d)) for d in (1, 2, 3)]
    for cp in enc:
        cp.start()

    eye = lax.broadcasted_iota(jnp.int32, (SEL, SEL), 0) == lax.broadcasted_iota(
        jnp.int32, (SEL, SEL), 1
    )
    inv_rows = inv_freq((SR, HD))

    def own_rope(c, carry):
        p = 2 * c + lax.div(s, 2)
        row = sel_ref[pl.ds(p, 1), :]
        col = jnp.sum(jnp.where(eye, jnp.broadcast_to(row, (SEL, SEL)), 0), axis=1, keepdims=True)
        pos_s[...] = jnp.broadcast_to(col + offs[p], (SEL, HD))
        mine = pos_s[pl.ds(pl.multiple_of(lax.rem(s, 2) * SR, SR), SR), :]
        cv, sv = rope_rows(mine.astype(F32) * inv_rows)
        rc[c] = cv
        rsn[c] = sv
        return carry

    def finish_missing():
        pos = lax.broadcasted_iota(jnp.int32, (PLEN, HD), 0).astype(F32)
        cosv, sinv = rope_rows(pos * inv_freq((PLEN, HD)))
        for cp in enc:
            cp.wait()
        summed = eb[...].astype(F32) + er[0].astype(F32) + er[1].astype(F32) + er[2].astype(F32)
        zb[t * POWN + POWN - 1, 0] = rotate(summed[:, :HD], cosv, sinv).astype(BF)
        zb[t * POWN + POWN - 1, 1] = summed[:, HD:].astype(BF)
        for way in range(2):
            z_out(POWN - 1, way)
        to_sib(0, 0, POWN - 1, POWN - 1)

    def p_send(c, d):
        rows = pl.ds(lax.rem(s + d, NS) * SR, SR)
        return remote(pb.at[c, rows], rb.at[c, d - 1], ps.at[c, d - 1], pr.at[c, d - 1], ydev(d))

    def project(c):
        def tile(n, carry):
            cols = pl.ds(pl.multiple_of(n * 256, 256), 256)
            total = jnp.zeros((CR, 256), F32)
            for slot, away in enumerate((0, 3, 1, 2)):
                owner = lax.rem(h + away, 4)
                wrows = pl.ds(pl.multiple_of(owner * FEAT, FEAT), FEAT)
                total += jnp.dot(
                    xb[slot, c * CR : (c + 1) * CR, :], wv[wrows, cols], preferred_element_type=F32
                )
            pb[c, :, cols] = total.astype(BF)
            return carry

        lax.fori_loop(0, COLS // 256, tile, 0)
        for d in (1, 2, 3):
            p_send(c, d).start()

    def f_rows(c, who):
        return fb.at[pl.ds(pl.multiple_of(c * CR + who * SR, SR), SR)]

    def f_send(c, d):
        slot = f_rows(c, s)
        return remote(slot, slot, fs.at[c, d - 1], fr.at[c, d - 1], ydev(d))

    def f_recv(c, d):
        slot = f_rows(c, lax.rem(s + NS - d, NS))
        return remote(slot, slot, fs.at[c, d - 1], fr.at[c, d - 1], ydev(d))

    def finish_rows(c):
        for d in (1, 2, 3):
            p_send(c, d).wait()
        mine = pb[c, pl.ds(pl.multiple_of(s * SR, SR), SR), :].astype(F32)
        x = mine + rb[c, 0].astype(F32) + rb[c, 1].astype(F32) + rb[c, 2].astype(F32)
        x = x.astype(BF).astype(F32)
        cv, sv = rc[c], rsn[c]
        rows = pl.ds(pl.multiple_of(c * CR + s * SR, SR), SR)
        fb[rows, :HD] = rotate(x[:, G * HD : (G + 1) * HD], cv, sv).astype(BF)
        fb[rows, HD:] = x[:, (G + 1) * HD :].astype(BF)
        for d in (1, 2, 3):
            f_send(c, d).start()
        q = jnp.concatenate(
            [rotate(x[:, g * HD : (g + 1) * HD], cv, sv) for g in range(G)], axis=0
        )
        qb[c] = jnp.transpose(q).astype(BF)

    turns = ((), (0,), (1, 2), (3, 4), (5,), (6, 7), (8, 9), (10, 11), (12,))
    for i in range(CH + 1):
        if i < CH:
            for cp in x_own(i):
                cp.wait()
            for cp in x_fwd(i):
                cp.start()
            if i + AHEAD < CH:
                for cp in x_own(i + AHEAD):
                    cp.start()
        if i == 0:
            lax.fori_loop(0, CH, own_rope, 0)
        if i >= 1:
            for cp in x_fwd(i - 1):
                cp.wait()
            project(i - 1)
        for n in turns[i]:
            z_service(n)
        if i == 1:
            finish_missing()
        if i >= LAG:
            finish_rows(i - LAG)
    for c in range(CH - LAG + 1, CH - 1):
        finish_rows(c)
    z_service(13)
    finish_rows(CH - 1)
    for d in range(1, NT):
        hits[d - 1].wait_send()
        other = hb.at[lax.rem(t + NT - d, NT)]
        remote(other, other, hs.at[d - 1], hr.at[d - 1], tdev[d]).wait_recv()
    hit_copy = pltpu.make_async_copy(hb, hsm, lsem.at[0])
    hit_copy.start()
    for cp in sib_back:
        cp.wait_recv()
    hit_copy.wait()

    kio = lax.broadcasted_iota(jnp.int32, (PLEN, SEL), 0)
    kcol = lax.broadcasted_iota(jnp.int32, (PLEN, 1), 0)
    count_row = lax.broadcasted_iota(jnp.int32, (VR - HD, PLEN), 0) == 0
    count_lane = lax.broadcasted_iota(jnp.int32, (VR - HD, PLEN), 1)

    def build(j, carry):
        pid = pid_ref[t, j]
        loc = loc_ref[pid]
        live = len_ref[pid]
        owner = lax.div(loc, POWN)
        slot = lax.rem(loc, POWN)
        gap = hsm[owner, 0, 0]
        place = jnp.where(slot == gap, POWN - 1, jnp.where(slot == POWN - 1, gap, slot))
        idx = owner * POWN + place
        half = pl.ds(pl.multiple_of(lax.rem(j, 2) * PLEN, PLEN), PLEN)
        pair = lax.div(j, 2)
        moved = rotate(zb[idx, 0].astype(F32), oc[pl.ds(j, 1), :], osn[pl.ds(j, 1), :])
        hot = (kio == sel_ref[pl.ds(j, 1), :]).astype(F32)
        chosen = jnp.max(hot, axis=1, keepdims=True) > 0.0
        rows = pl.ds(pl.multiple_of(j * SEL, SEL), SEL)
        fresh = jnp.dot(hot.astype(BF), fb[rows, :], preferred_element_type=F32)
        keys = jnp.where(chosen, fresh[:, :HD], moved)
        keys = jnp.where(kcol < live, keys, keys[0:1, :])
        ktab[pair, half, :] = keys.astype(BF)
        vals = jnp.where(chosen, fresh[:, HD:], zb[idx, 1].astype(F32))
        vals = jnp.where(kcol < live, vals, 0.0)
        vtab[pair, 0:HD, half] = jnp.transpose(vals).astype(BF)
        vtab[pair, HD:VR, half] = jnp.where(count_row & (count_lane < live), 1.0, 0.0).astype(BF)
        return carry

    def o_ref(c, who):
        rows = pl.ds(pl.multiple_of(lax.rem(who, 2) * SR, SR), SR)
        return out_ref.at[c % 2 * 2 + lax.div(who, 2), rows]

    def o_copy(c, who):
        return remote(ob.at[c], o_ref(c, who), os_.at[c], or_.at[c % 2, who], {"serve": c // 2})

    pcol = lax.broadcasted_iota(jnp.int32, (2 * PLEN, 1), 0)

    def soft_step(*steps):
        scores = [
            jnp.dot(ktab[pair], qb[c], preferred_element_type=F32) for _, c, pair, _ in steps
        ]
        for (slot, _, pair, lim), sc in zip(steps, scores):
            if lim is not None:
                sc = jnp.where(pcol <= lim, sc, -jnp.inf)
            m_old = m_s[slot]
            m_new = jnp.maximum(m_old, jnp.max(sc, axis=0, keepdims=True))
            alpha = jnp.exp2((m_old - m_new) * EXP_SCALE)
            e = jnp.exp2((sc - m_new) * EXP_SCALE).astype(BF)
            m_s[slot] = m_new
            acc_s[slot] = acc_s[slot] * alpha + jnp.dot(
                vtab[pair], e, preferred_element_type=F32
            )

    def build_pair(c):
        for d in (1, 2, 3):
            f_send(c, d).wait_send()
            f_recv(c, d).wait_recv()
        lax.fori_loop(2 * c, 2 * c + 2, build, 0)

    late = lax.div(s, 2)

    def limits(c):
        row = sel_ref[pl.ds(2 * c + late, 1), :]
        lim = jnp.where(lax.rem(s, 2) == 0, row[:, :SR], row[:, SR:])
        return jnp.concatenate([lim] * G, axis=1) + late * PLEN

    def deliver(c, acc):
        o = jnp.transpose(acc[0:HD, :] / acc[HD : HD + 1, :])
        for g in range(G):
            ob[c, :, g * HD : (g + 1) * HD] = o[g * SR : (g + 1) * SR].astype(BF)

        @pl.when(s == c // 2)
        def _():
            rows = pl.ds(pl.multiple_of(lax.rem(s, 2) * SR, SR), SR)
            out_ref[c % 2 * 2 + lax.div(s, 2), rows, :] = ob[c]

        @pl.when(s != c // 2)
        def _():
            o_copy(c, s).start()

    def clear():
        m_s[...] = jnp.full((8, 1, G * SR), -jnp.inf, F32)
        acc_s[...] = jnp.zeros((8, VR, G * SR), F32)

    def attend(first, last):
        chunks = range(first, last + 1)
        clear()

        def common(pair, carry):
            soft_step(*[(c - first, c, pair, None) for c in chunks])
            return carry

        lax.fori_loop(0, first, common, 0)
        for pair in chunks:
            build_pair(pair)
            soft_step(
                *[
                    (c - first, c, pair, limits(c) if c == pair else None)
                    for c in range(pair, last + 1)
                ]
            )
            deliver(pair, acc_s[pair - first])

    attend(0, 7)
    for cp in sends:
        cp.wait_send()

    for c in range(CH):

        @pl.when(s != c // 2)
        def _():
            o_copy(c, s).wait_send()

    for c in range(2):
        for who in range(NS):

            @pl.when(s != who)
            def _():
                o_copy(c, who).wait_recv()


def local(
    passage_ids, location, passage_len, hit, sel_index, sel_hidden, miss_hidden, w_qkv, cache
):
    smem = pl.BlockSpec(memory_space=pltpu.SMEM)
    vmem = pl.BlockSpec(memory_space=pltpu.VMEM)
    hbm = pl.BlockSpec(memory_space=pl.ANY)
    dma = pltpu.SemaphoreType.DMA
    out = pl.pallas_call(
        kernel,
        out_shape=jax.ShapeDtypeStruct((NPAS // NS, SEL, G * HD), BF),
        in_specs=[smem, smem, smem, smem, vmem, hbm, hbm, hbm, hbm],
        out_specs=vmem,
        scratch_shapes=[
            pltpu.VMEM((4 * FEAT, COLS), BF),
            pltpu.VMEM((PLEN, 4 * FEAT), BF),
            pltpu.VMEM((4, ROWS, FEAT), BF),
            pltpu.VMEM((POWN, 2, PLEN, HD), BF),
            pltpu.VMEM((NT * POWN, 2, PLEN, HD), BF),
            pltpu.VMEM((NT, 1, HD), jnp.int32),
            pltpu.SMEM((NT, 1, HD), jnp.int32),
            pltpu.VMEM((PLEN, 2 * HD), BF),
            pltpu.VMEM((3, PLEN, 2 * HD), BF),
            pltpu.VMEM((CH, CR, COLS), BF),
            pltpu.VMEM((CH, 3, SR, COLS), BF),
            pltpu.VMEM((ROWS, 2 * HD), BF),
            pltpu.VMEM((CH, HD, G * SR), BF),
            pltpu.VMEM((NPAS // 2, 2 * PLEN, HD), BF),
            pltpu.VMEM((NPAS // 2, VR, 2 * PLEN), BF),
            pltpu.VMEM((CH, SR, G * HD), BF),
            pltpu.VMEM((SEL, HD), jnp.int32),
            pltpu.SMEM((NPAS,), jnp.int32),
            pltpu.VMEM((NPAS, HD), F32),
            pltpu.VMEM((NPAS, HD), F32),
            pltpu.VMEM((CH, SR, HD), F32),
            pltpu.VMEM((CH, SR, HD), F32),
            pltpu.VMEM((8, VR, G * SR), F32),
            pltpu.VMEM((8, 1, G * SR), F32),
            dma((4,)),
            dma((NT - 1,)),
            dma((NT - 1,)),
            dma((4, CH)),
            dma((4, CH)),
            dma((3,)),
            dma((3,)),
            dma((2, 14)),
            dma((2, 14)),
            dma((32,)),
            dma((32,)),
            dma((CH, 3)),
            dma((CH, 3)),
            dma((CH, 3)),
            dma((CH, 3)),
            dma((CH,)),
            dma((2, NS)),
        ],
        compiler_params=pltpu.CompilerParams(
            collective_id=0, has_side_effects=True, vmem_limit_bytes=56 * 2**20
        ),
        cost_estimate=pl.CostEstimate(
            flops=10 * 10**9, bytes_accessed=9 * 2**20, transcendentals=8 * 2**20
        ),
        name="blended_attention",
    )(
        passage_ids,
        location,
        passage_len,
        hit,
        sel_index[0],
        sel_hidden[0],
        miss_hidden[0],
        w_qkv,
        cache,
    )
    return out[None]


def solution(mesh):
    in_specs = (
        P(),
        P(),
        P(),
        P("tier"),
        P("tier", None, None),
        P("tier", None, ("serve", "head")),
        P("tier", None, "serve"),
        P("serve", "head"),
        P("tier", None, None, "head"),
    )
    out_specs = P("tier", "serve", None, "head")
    return jax.shard_map(local, mesh=mesh, in_specs=in_specs, out_specs=out_specs, check_vma=False)
```
